256 devices in a mesh: clip: 8 (over x, y_hi), sy: 8 (over z), sx: 4 (over y_lo, core).
Axes of the slice: x: 4, y: 4 (y_hi: 2, y_lo: 2; y = y_hi * 2 + y_lo), z: 8, core: 2. Of those that a mesh axis runs over, the one named last changes fastest.
Arguments:
- queries: bfloat16 [8, 4, 64, 32, 1536], P('clip', None, 'sy', 'sx'), may hold values from -12 to 12
- keys: bfloat16 [8, 4, 64, 32, 1536], P('clip', None, 'sy', 'sx'), may hold values from -9 to 9
- values: bfloat16 [8, 4, 64, 32, 1536], P('clip', None, 'sy', 'sx'), may hold values from -6 to 6
- cache: bfloat16 [32, 8, 4, 2, 64, 1536], P('clip', 'sy', 'sx'), may hold values from -7 to 7
- ctx_owner: int32 [8, 8, 4, 8], P('clip', 'sy', 'sx'), may hold values from 0 to 7, as said below
- ctx_slot: int32 [8, 8, 4, 8], P('clip', 'sy', 'sx'), may hold values from 0 to 3
- span_count: int32 [8], P('clip'), may hold values from 2 to 4
Outputs:
- attended: bfloat16 [8, 4, 64, 32, 1536], P('clip', None, 'sy', 'sx')
The draws below stay inside these ranges and needn't reach their ends.
Inputs may be any that keep to these rules, and one draw needn't show every extreme that they name: `ctx_owner`: entries 2 * i to 2 * i + 1 of every tile's list name one owner, and different i name different owners.
All inputs are finite; a program needn't handle non-finite values.
Results may differ from the reference program's by a relative error of at most 0.0033.
Values may be sent and summed in bfloat16 or wider, within the bound.
A program may use at most 128 MiB of HBM per device.

```python
import math
import jax
import jax.numpy as jnp
from jax import lax

HEAD = 128
HD = 1536
FR = 4
TH = 8
TW = 8
REACH = 3
BLK = 64
CTX = 8
BPC = 2
SPANS = 4
NBLK_DEV = 4
MOST = 2
CLIPS = 8
CACHE_BLOCKS = 32
GH = 64
GW = 32
N_CLIP = 8
N_SY = 8
N_SX = 4


def draw_queries(key, part):
    key = jax.random.fold_in(key, 11)
    grid_shape = (CLIPS, FR, GH, GW, HD)
    drawn = jnp.clip(jax.random.normal(key, grid_shape, jnp.float32) * 1.5, -9.0, 9.0)
    return drawn.astype(jnp.bfloat16)


def draw_keys(key, part):
    key = jax.random.fold_in(key, 12)
    grid_shape = (CLIPS, FR, GH, GW, HD)
    drawn = jnp.clip(jax.random.normal(key, grid_shape, jnp.float32) * 1.5, -9.0, 9.0)
    return drawn.astype(jnp.bfloat16)


def draw_ctx_owner(key, part):
    key = jax.random.fold_in(key, 31)
    hot_owner = jax.random.randint(key, (N_SY, N_SX), 0, N_CLIP)
    grid_shape = (CLIPS, N_SY, N_SX, CTX)
    clip_place = lax.broadcasted_iota(jnp.int32, grid_shape, 0)
    entry_place = lax.broadcasted_iota(jnp.int32, grid_shape, 3)
    owners = (hot_owner[None, :, :, None] + clip_place % 2 + entry_place // MOST) % N_CLIP
    return owners.astype(jnp.int32)


def draw_span_count(key, part):
    key = jax.random.fold_in(key, 41)
    first_key, second_key = jax.random.split(key)
    counts_drawn = jax.random.randint(first_key, (CLIPS,), 2, SPANS + 1)
    fullest = jax.random.randint(second_key, (), 0, CLIPS)
    counts_drawn = jnp.where(jnp.arange(CLIPS) == fullest, SPANS, counts_drawn)
    return counts_drawn.astype(jnp.int32)


def with_ends(array, key, least, top_value):
    index_at = [jax.random.randint(jax.random.fold_in(key, axis), (), 0, length) for axis, length in enumerate(array.shape)]
    widest = array.shape.index(max(array.shape))
    beside = index_at[:widest] + [(index_at[widest] + 1) % array.shape[widest]] + index_at[widest + 1:]
    return array.at[tuple(index_at)].set(least).at[tuple(beside)].set(top_value)


def shard_levels(rng, dims, cuts, smallest, largest):
    loudness, own = 1.0, jax.random.fold_in(rng, 6)
    for axis_at, parts in cuts:
        draws = jnp.exp(jax.random.uniform(jax.random.fold_in(own, axis_at), (parts,), jnp.float32, smallest / len(cuts), largest / len(cuts)))
        loudness = loudness * jnp.repeat(draws, dims[axis_at] // parts).reshape([-1 if axis == axis_at else 1 for axis in range(len(dims))])
    return loudness


def scatter_about(key, extent, deviation, reach, cuts=(), kind=jnp.bfloat16):
    gain = shard_levels(key, extent, cuts, -0.22, 0.18) if cuts else 1.0
    values = jax.random.normal(key, extent, jnp.float32) * deviation * gain
    return jnp.minimum(jnp.maximum(values, -reach), reach).astype(kind)


def setup_inputs(seed: int = 0) -> dict:
    splits = jax.random.split(jax.random.key(seed), 8)
    queries = draw_queries(jax.random.fold_in(splits[7], 71), 0)
    keys = draw_keys(jax.random.fold_in(splits[7], 71), 0)
    values = scatter_about(splits[2], (CLIPS, FR, GH, GW, HD), 1.0, 6.0, ((0, 8), (2, 8), (3, 4)))
    cache = scatter_about(splits[3], (CACHE_BLOCKS, N_SY, N_SX, 2, BLK, HD), 1.2, 7.0, ((0, 8), (1, 8), (2, 4)))
    ctx_owner = draw_ctx_owner(jax.random.fold_in(splits[7], 71), 0)
    ctx_slot = with_ends(jax.random.randint(splits[5], (CLIPS, N_SY, N_SX, CTX), 0, NBLK_DEV), jax.random.fold_in(splits[5], 1), 0, NBLK_DEV - 1).astype(jnp.int32)
    span_count = draw_span_count(jax.random.fold_in(splits[7], 71), 0)
    return dict(queries=queries, keys=keys, values=values, cache=cache, ctx_owner=ctx_owner, ctx_slot=ctx_slot, span_count=span_count)


def window_mask(row_first, grid_rows, col_first, grid_cols, tile_rows, tile_cols, frames):
    query_rows = jnp.arange(tile_rows, dtype=jnp.int32)
    key_rows = jnp.arange(tile_rows + 2 * REACH, dtype=jnp.int32) - REACH
    near_rows = (jnp.abs(query_rows[:, None] - key_rows[None, :]) <= REACH) & (key_rows[None, :] + row_first >= 0) & (key_rows[None, :] + row_first < grid_rows)
    query_cols = jnp.arange(tile_cols, dtype=jnp.int32)
    key_cols = jnp.arange(tile_cols + 2 * REACH, dtype=jnp.int32) - REACH
    near_cols = (jnp.abs(query_cols[:, None] - key_cols[None, :]) <= REACH) & (key_cols[None, :] + col_first >= 0) & (key_cols[None, :] + col_first < grid_cols)
    plane_mask = near_rows[:, None, :, None] & near_cols[None, :, None, :]
    plane_mask = plane_mask.reshape(tile_rows * tile_cols, -1)
    full_mask = jnp.broadcast_to(plane_mask[None, :, None, :], (frames, tile_rows * tile_cols, frames, plane_mask.shape[1]))
    return full_mask.reshape(frames * tile_rows * tile_cols, -1)

def attend(query_flat, key_flat, value_flat, allowed):
    rows_q = query_flat.shape[0]
    features = query_flat.shape[1]
    head_count = features // HEAD
    query_heads = query_flat.astype(jnp.float32).reshape(rows_q, head_count, HEAD)
    key_heads = key_flat.astype(jnp.float32).reshape(-1, head_count, HEAD)
    value_heads = value_flat.astype(jnp.float32).reshape(-1, head_count, HEAD)
    scores = jnp.einsum('qhd,khd->hqk', query_heads, key_heads, precision=lax.Precision.HIGHEST) * (1.0 / math.sqrt(HEAD))
    scores = jnp.where(allowed[None], scores, jnp.float32(-1e+30))
    highest = lax.optimization_barrier(jnp.max(scores, axis=2, keepdims=True))
    unnormed = jnp.exp(scores - highest)
    totals = lax.optimization_barrier(jnp.sum(unnormed, axis=2))
    weights = lax.optimization_barrier(unnormed.astype(jnp.bfloat16)).astype(jnp.float32)
    mixture = jnp.einsum('hqk,khd->qhd', weights, value_heads, precision=lax.Precision.HIGHEST)
    mixture = mixture / jnp.transpose(totals)[:, :, None]
    return mixture.reshape(rows_q, features).astype(jnp.bfloat16)

def reference(queries, keys, values, cache, ctx_owner, ctx_slot, span_count):
    features = queries.shape[4]
    grid_rows = queries.shape[2]
    grid_cols = queries.shape[3]
    widths = ((0, 0), (0, 0), (REACH, REACH), (REACH, REACH), (0, 0))
    padded_keys = jnp.pad(keys, widths)
    padded_values = jnp.pad(values, widths)
    zero_index = jnp.zeros((), jnp.int32)

    def one_tile(tile_index):
        clip_index = tile_index // (N_SY * N_SX)
        tile_row = tile_index // N_SX % N_SY
        tile_col = tile_index % N_SX
        row_first = (tile_row * TH).astype(jnp.int32)
        col_first = (tile_col * TW).astype(jnp.int32)
        starts = (clip_index, zero_index, row_first, col_first, zero_index)
        query_flat = lax.dynamic_slice(queries, starts, (1, FR, TH, TW, features)).reshape(-1, features)
        key_local = lax.dynamic_slice(padded_keys, starts, (1, FR, TH + 2 * REACH, TW + 2 * REACH, features)).reshape(-1, features)
        value_local = lax.dynamic_slice(padded_values, starts, (1, FR, TH + 2 * REACH, TW + 2 * REACH, features)).reshape(-1, features)
        block_ids = (ctx_owner[clip_index, tile_row, tile_col] * NBLK_DEV + ctx_slot[clip_index, tile_row, tile_col]).astype(jnp.int32)
        fetched = cache[block_ids, tile_row, tile_col]
        live_mask = jnp.arange(CTX, dtype=jnp.int32) // BPC < span_count[clip_index]
        key_flat = jnp.concatenate([key_local, fetched[:, 0].reshape(-1, features)], 0)
        value_flat = jnp.concatenate([value_local, fetched[:, 1].reshape(-1, features)], 0)
        local_mask = window_mask(row_first, grid_rows, col_first, grid_cols, TH, TW, FR)
        context_mask = jnp.broadcast_to(jnp.repeat(live_mask, BLK)[None, :], (local_mask.shape[0], CTX * BLK))
        allowed = jnp.concatenate([local_mask, context_mask], 1)
        return attend(query_flat, key_flat, value_flat, allowed).reshape(FR, TH, TW, features)
    tiles = lax.map(one_tile, jnp.arange(CLIPS * N_SY * N_SX, dtype=jnp.int32))
    tiles = tiles.reshape(CLIPS, N_SY, N_SX, FR, TH, TW, features)
    tiles = jnp.transpose(tiles, (0, 3, 1, 4, 2, 5, 6))
    return tiles.reshape(CLIPS, FR, GH, GW, features)
```

```python
import functools
import math

import jax
import jax.numpy as jnp
from jax import lax
from jax.experimental import pallas as pl
from jax.experimental.pallas import tpu as pltpu
from jax.sharding import PartitionSpec as P

HEAD = 128
HEADS = 12
HD = HEAD * HEADS
REACH = 3
BLK = 64
BPC = 2
CTX = 8
SLOTS = 4
FRAMES = 4
QN = 256
STRIP = 192
CHUNKS = 3
CW = HD // CHUNKS
LEAD = 2
FIRST_OWN = 7
NONE = -1e30
FLOOR = -1e29
RATE = math.log2(math.e) / math.sqrt(HEAD)
TWICE = 1.0 / RATE
MESH = pl.DeviceIdType.MESH
NT = (((1,), (1,)), ((), ()))
TN = (((0,), (0,)), ((), ()))


def dot(a, b, dims):
    return lax.dot_general(a, b, dims, preferred_element_type=jnp.float32)


def kernel(
    owner_ref, slot_ref, span_ref, q_hbm, k_hbm, v_hbm, cache_hbm, out_hbm,
    land, q_own, q_far, kv_own, kv_up, kv_dn, strip_out, strip_in, select, mask,
    bias_own, bias_out, bias_far, part_out, part_in, out_buf,
    cache_sem, q_sem, kv_sem, own_ss, own_rs, fwd_ss, fwd_rs, qs, qr, ps, pr,
    bias_ss, bias_rs, row_ss, row_rs, col_ss, col_rs, out_sem,
):
    clip = lax.axis_index("clip")
    sy = lax.axis_index("sy")
    sx = lax.axis_index("sx")
    rows_n = lax.axis_size("sy")
    cols_n = lax.axis_size("sx")
    x = clip // 2
    yh = clip % 2
    x_next = (lax.rem(clip + 2, 8), sy, sx)
    x_prev = (lax.rem(clip + 6, 8), sy, sx)
    across = (clip + 1 - 2 * yh, sy, sx)
    row_next = (clip, lax.rem(sy + 1, rows_n), sx)
    row_prev = (clip, lax.rem(sy + rows_n - 1, rows_n), sx)
    col_next = (clip, sy, lax.rem(sx + 1, cols_n))
    col_prev = (clip, sy, lax.rem(sx + cols_n - 1, cols_n))

    def lanes(h, width=HEAD):
        return pl.ds(pl.multiple_of(h * width, HEAD), width)

    def cache_copy(h):
        return pltpu.make_async_copy(cache_hbm.at[:, :, :, lanes(h)], land.at[h, 0], cache_sem.at[h])

    def q_copy(h):
        return pltpu.make_async_copy(q_hbm.at[:, lanes(h)], q_own.at[h], q_sem.at[h])

    def out_copy(h):
        return pltpu.make_async_copy(out_buf.at[h], out_hbm.at[:, lanes(h)], out_sem.at[h])

    k_copy = pltpu.make_async_copy(k_hbm, kv_own.at[0], kv_sem.at[0])
    v_copy = pltpu.make_async_copy(v_hbm, kv_own.at[1], kv_sem.at[1])

    def remote(src, dst, ss, rs, device):
        return pltpu.make_async_remote_copy(
            src_ref=src, dst_ref=dst, send_sem=ss, recv_sem=rs, device_id=device, device_id_type=MESH
        )

    def own_send(h, way):
        return remote(
            land.at[h, 0], land.at[h, 1 + way], own_ss.at[way, h], own_rs.at[way, h], (x_next, x_prev)[way]
        )

    def forward(h, way):
        half = pl.ds(2 * way, 2)
        return remote(
            land.at[h, 1 + way, half], land.at[h, 3, half], fwd_ss.at[way, h], fwd_rs.at[way, h],
            (x_next, x_prev)[way],
        )

    def q_send(h):
        return remote(q_own.at[h], q_far.at[h], qs.at[h], qr.at[h], across)

    def part_send(h):
        return remote(part_out.at[h], part_in.at[h], ps.at[h], pr.at[h], across)

    bias_send = remote(bias_out, bias_far, bias_ss, bias_rs, across)

    def row_send(c, way):
        rows = pl.ds(32 * (1 - way), 32)
        return remote(
            kv_own.at[:, :, rows, lanes(c, CW)], (kv_up, kv_dn)[way].at[c], row_ss.at[way, c], row_rs.at[way, c],
            (row_next, row_prev)[way],
        )

    def col_send(c, way):
        return remote(
            strip_out.at[way, c], strip_in.at[way, c], col_ss.at[way, c], col_rs.at[way, c],
            (col_next, col_prev)[way],
        )

    row_has = (sy > 0, sy < rows_n - 1)
    row_to = (sy < rows_n - 1, sy > 0)
    col_has = (sx > 0, sx < cols_n - 1)
    col_to = (sx < cols_n - 1, sx > 0)

    def start_local(h, carry):
        cache_copy(h).start()
        q_copy(h).start()
        return carry

    barrier = pltpu.get_barrier_semaphore()
    for device in (x_next, x_prev, across, row_next, row_prev, col_next, col_prev):
        pl.semaphore_signal(barrier, inc=1, device_id=device, device_id_type=MESH)
    k_copy.start()
    v_copy.start()
    lax.fori_loop(0, HEADS, start_local, 0)

    place = lax.broadcasted_iota(jnp.int32, (16, QN), 0)
    source = place >> 2
    step = jnp.where(source == 0, 0, jnp.where(source == 1, 3, jnp.where(source == 2, 1, 2)))
    base = ((x + step) & 3) * (2 * SLOTS) + (place & 3)
    for ref, half in ((bias_own, yh), (bias_out, 1 - yh)):
        target = base + half * SLOTS
        count = jnp.zeros((16, QN), jnp.int32)
        for j in range(CTX):
            listed = owner_ref[j] * SLOTS + slot_ref[j]
            listed = jnp.where(j // BPC < span_ref[0], listed, -1)
            count = count + jnp.where(target == listed, 1, 0)
        ref[...] = jnp.where(count == 0, NONE, jnp.where(count == 1, 0.0, TWICE)).astype(jnp.float32)

    pl.semaphore_wait(barrier, 7)
    for h in range(LEAD):
        cache_copy(h).wait()
        own_send(h, 0).start()
        own_send(h, 1).start()
        q_copy(h).wait()
        q_send(h).start()
        if h == 0:
            bias_send.start()
    k_copy.wait()
    v_copy.wait()
    for c in range(CHUNKS):
        for way in range(2):
            pl.when(row_to[way])(row_send(c, way).start)

    for way, ref in ((0, kv_up), (1, kv_dn)):

        @pl.when(jnp.logical_not(row_has[way]))
        def _():
            ref[...] = jnp.zeros_like(ref)

    for way in range(2):

        @pl.when(jnp.logical_not(col_has[way]))
        def _():
            strip_in[way] = jnp.zeros(strip_in.shape[1:], strip_in.dtype)

    strip_row = lax.broadcasted_iota(jnp.int32, (STRIP, 512), 0)
    from_row = lax.broadcasted_iota(jnp.int32, (STRIP, 512), 1)
    frame = (strip_row >> 4) & 3
    height = strip_row & 15
    for way in range(2):
        column = (strip_row >> 6) + (5 if way == 0 else 0)
        wanted = jnp.where(
            height < 4,
            256 + frame * 32 + height * 8,
            jnp.where(height < 12, frame * 64 + (height - 4) * 8, 384 + frame * 32 + (height - 12) * 8),
        )
        select[way] = jnp.where(wanted + column == from_row, 1.0, 0.0).astype(jnp.bfloat16)

    def mask_part(first, count, row_col):
        r = lax.broadcasted_iota(jnp.int32, (count, QN), 0)
        query = lax.broadcasted_iota(jnp.int32, (count, QN), 1)
        row, col = row_col(r)
        down = row - ((query >> 3) & 7)
        right = col - (query & 7)
        row_at = row + sy * 8
        col_at = col + sx * 8
        near = (down <= REACH) & (down >= -REACH) & (right <= REACH) & (right >= -REACH)
        inside = (row_at >= 0) & (row_at < rows_n * 8) & (col_at >= 0) & (col_at < cols_n * 8)
        mask[first : first + count, :] = jnp.where(near & inside, 0.0, NONE).astype(jnp.float32)

    mask_part(0, 256, lambda r: ((r >> 3) & 7, r & 7))
    mask_part(256, 128, lambda r: (((r >> 3) & 3) - 4, r & 7))
    mask_part(384, 128, lambda r: (((r >> 3) & 3) + 8, r & 7))
    mask_part(512, STRIP, lambda r: ((r & 15) - 4, (r >> 6) - 3))
    mask_part(512 + STRIP, STRIP, lambda r: ((r & 15) - 4, (r >> 6) + 8))

    def ring_scores(h, query, bias):
        scores, highest = [], jnp.full((1, QN), FLOOR, jnp.float32)
        for r in range(4):
            s = dot(land[h, r, :, 0].reshape(QN, HEAD), query, NT)
            for b in range(4):
                top = jnp.max(s[b * BLK : (b + 1) * BLK], axis=0, keepdims=True)
                highest = jnp.maximum(highest, top + bias[4 * r + b : 4 * r + b + 1])
            scores.append(s)
        return scores, highest

    def ring_sums(h, scores, highest, bias, total, mixed):
        for r in range(4):
            shift = [highest - bias[4 * r + b : 4 * r + b + 1] for b in range(4)]
            p = jnp.concatenate(
                [jnp.exp2((scores[r][b * BLK : (b + 1) * BLK] - shift[b]) * RATE) for b in range(4)], 0
            )
            total = total + jnp.sum(p, axis=0, keepdims=True)
            mixed = mixed + dot(land[h, r, :, 1].reshape(QN, HEAD), p.astype(jnp.bfloat16), TN)
        return total, mixed

    def attend_far(h):
        bias = bias_far[...]
        scores, highest = ring_scores(h, q_far[h], bias)
        highest = highest.astype(jnp.bfloat16).astype(jnp.float32)
        total, mixed = ring_sums(
            h, scores, highest, bias, jnp.zeros((1, QN), jnp.float32), jnp.zeros((HEAD, QN), jnp.float32)
        )
        coarse = total.astype(jnp.bfloat16).astype(jnp.float32)
        row = lax.broadcasted_iota(jnp.int32, (16, QN), 0)
        stats = jnp.where(row == 0, highest, jnp.where(row == 1, coarse, total - coarse))
        part_out[h, :HEAD] = mixed.astype(jnp.bfloat16)
        part_out[h, HEAD:] = stats.astype(jnp.bfloat16)

    def attend_own(h):
        query = q_own[h]
        bias = bias_own[...]
        c = h // (HEADS // CHUNKS)
        here = lanes(h - c * (HEADS // CHUNKS))

        def pieces(kv):
            own = kv_own[kv, :, :, lanes(h)].reshape(QN, HEAD)
            up = kv_up[c, kv, :, :, here].reshape(128, HEAD)
            dn = kv_dn[c, kv, :, :, here].reshape(128, HEAD)
            left = strip_in[0, c, kv, :, here]
            right = strip_in[1, c, kv, :, here]
            return own, jnp.concatenate([up, dn], 0), jnp.concatenate([left, right], 0)

        scores, highest = ring_scores(h, query, bias)
        near, first = [], 0
        for piece in pieces(0):
            s = dot(piece, query, NT) + mask[first : first + piece.shape[0], :]
            first += piece.shape[0]
            highest = jnp.maximum(highest, jnp.max(s, axis=0, keepdims=True))
            near.append(s)
        total, mixed = ring_sums(
            h, scores, highest, bias, jnp.zeros((1, QN), jnp.float32), jnp.zeros((HEAD, QN), jnp.float32)
        )
        for piece, s in zip(pieces(1), near):
            p = jnp.exp2((s - highest) * RATE)
            total = total + jnp.sum(p, axis=0, keepdims=True)
            mixed = mixed + dot(piece, p.astype(jnp.bfloat16), TN)
        part_send(h).wait_recv()
        stats = part_in[h, HEAD:].astype(jnp.float32)
        far_highest, far_total = stats[0:1], stats[1:2] + stats[2:3]
        top = jnp.maximum(highest, far_highest)
        here_scale = jnp.exp2((highest - top) * RATE)
        far_scale = jnp.exp2((far_highest - top) * RATE)
        inverse = 1.0 / (total * here_scale + far_total * far_scale)
        result = mixed * (here_scale * inverse) + part_in[h, :HEAD].astype(jnp.float32) * (far_scale * inverse)
        out_buf[h] = result.T.astype(jnp.bfloat16)
        out_copy(h).start()

    def make_strips(c):
        for way in range(2):
            pl.when(row_has[way])(row_send(c, way).wait_recv)
        for kv in range(2):
            tile = kv_own[kv, :, :, lanes(c, CW)].reshape(QN, CW)
            halo = jnp.concatenate([kv_up[c, kv].reshape(128, CW), kv_dn[c, kv].reshape(128, CW)], 0)
            for way in range(2):
                packed = jnp.dot(select[way, :, :QN], tile, preferred_element_type=jnp.float32)
                packed = packed + jnp.dot(select[way, :, QN:], halo, preferred_element_type=jnp.float32)
                strip_out[way, c, kv] = packed.astype(jnp.bfloat16)
        for way in range(2):
            pl.when(col_to[way])(col_send(c, way).start)

    def ring_step(h, carry):
        @pl.when(h < HEADS)
        def _():
            for way in range(2):
                own_send(h, way).wait_recv()
                forward(h, way).start()

        @pl.when(h + LEAD < HEADS)
        def _():
            cache_copy(h + LEAD).wait()
            own_send(h + LEAD, 0).start()
            own_send(h + LEAD, 1).start()
            q_copy(h + LEAD).wait()
            q_send(h + LEAD).start()

        @pl.when((h >= 2) & (h < 2 + CHUNKS))
        def _():
            make_strips(h - 2)

        @pl.when(h >= 1)
        def _():
            for way in range(2):
                forward(h - 1, way).wait_recv()
            q_send(h - 1).wait_recv()
            pl.when(h == 1)(bias_send.wait_recv)
            attend_far(h - 1)
            part_send(h - 1).start()

        @pl.when(h >= FIRST_OWN)
        def _():
            first = 2 * (h - FIRST_OWN)

            @pl.when(lax.rem(first, HEADS // CHUNKS) == 0)
            def _():
                for way in range(2):
                    pl.when(col_has[way])(col_send(first // (HEADS // CHUNKS), way).wait_recv)

            def own_step(i, carry):
                attend_own(first + i)
                return carry

            lax.fori_loop(0, 2, own_step, 0)

        return carry

    lax.fori_loop(0, HEADS + 1, ring_step, 0)

    def finish(h, carry):
        for way in range(2):
            own_send(h, way).wait_send()
            forward(h, way).wait_send()
        q_send(h).wait_send()
        part_send(h).wait_send()
        out_copy(h).wait()
        return carry

    lax.fori_loop(0, HEADS, finish, 0)
    bias_send.wait_send()
    for c in range(CHUNKS):
        for way in range(2):
            pl.when(row_to[way])(row_send(c, way).wait_send)
            pl.when(col_to[way])(col_send(c, way).wait_send)


def per_device(queries, keys, values, cache, ctx_owner, ctx_slot, span_count):
    bf16, f32, dma = jnp.bfloat16, jnp.float32, pltpu.SemaphoreType.DMA
    smem = pl.BlockSpec(memory_space=pltpu.SMEM)
    anywhere = pl.BlockSpec(memory_space=pl.ANY)
    attended = pl.pallas_call(
        kernel,
        out_shape=jax.ShapeDtypeStruct((QN, HD), bf16),
        in_specs=[smem] * 3 + [anywhere] * 4,
        out_specs=anywhere,
        scratch_shapes=[
            pltpu.VMEM((HEADS, 4, SLOTS, 2, BLK, HEAD), bf16),
            pltpu.VMEM((HEADS, QN, HEAD), bf16),
            pltpu.VMEM((HEADS, QN, HEAD), bf16),
            pltpu.VMEM((2, FRAMES, 64, HD), bf16),
            pltpu.VMEM((CHUNKS, 2, FRAMES, 32, CW), bf16),
            pltpu.VMEM((CHUNKS, 2, FRAMES, 32, CW), bf16),
            pltpu.VMEM((2, CHUNKS, 2, STRIP, CW), bf16),
            pltpu.VMEM((2, CHUNKS, 2, STRIP, CW), bf16),
            pltpu.VMEM((2, STRIP, 512), bf16),
            pltpu.VMEM((512 + 2 * STRIP, QN), f32),
            pltpu.VMEM((16, QN), f32),
            pltpu.VMEM((16, QN), f32),
            pltpu.VMEM((16, QN), f32),
            pltpu.VMEM((HEADS, HEAD + 16, QN), bf16),
            pltpu.VMEM((HEADS, HEAD + 16, QN), bf16),
            pltpu.VMEM((HEADS, QN, HEAD), bf16),
            dma((HEADS,)), dma((HEADS,)), dma((2,)),
            dma((2, HEADS)), dma((2, HEADS)), dma((2, HEADS)), dma((2, HEADS)),
            dma((HEADS,)), dma((HEADS,)), dma((HEADS,)), dma((HEADS,)),
            dma, dma,
            dma((2, CHUNKS)), dma((2, CHUNKS)), dma((2, CHUNKS)), dma((2, CHUNKS)),
            dma((HEADS,)),
        ],
        compiler_params=pltpu.CompilerParams(
            collective_id=0, has_side_effects=True, vmem_limit_bytes=60 * 2**20
        ),
        cost_estimate=pl.CostEstimate(flops=4 * QN * 2944 * HD, bytes_accessed=6 * 2**20, transcendentals=QN * 2944 * HEADS),
        name="span_attention",
    )(
        ctx_owner.reshape(-1),
        ctx_slot.reshape(-1),
        span_count.reshape(-1),
        queries.reshape(QN, HD),
        keys.reshape(FRAMES, 64, HD),
        values.reshape(FRAMES, 64, HD),
        cache.reshape(SLOTS, 2, BLK, HD),
    )
    return attended.reshape(queries.shape)


def solution(mesh):
    placed = (
        P("clip", None, "sy", "sx", None),
        P("clip", None, "sy", "sx", None),
        P("clip", None, "sy", "sx", None),
        P("clip", "sy", "sx", None, None, None),
        P("clip", "sy", "sx", None),
        P("clip", "sy", "sx", None),
        P("clip"),
    )
    return jax.shard_map(
        per_device,
        mesh=mesh,
        in_specs=placed,
        out_specs=P("clip", None, "sy", "sx", None),
        check_vma=False,
    )
```

```python
import functools
import math

import jax
import jax.numpy as jnp
from jax import lax
from jax.experimental import pallas as pl
from jax.experimental.pallas import tpu as pltpu
from jax.sharding import PartitionSpec as P

HEAD = 128
HEADS = 12
HD = HEAD * HEADS
REACH = 3
BLK = 64
BPC = 2
CTX = 8
SLOTS = 4
FRAMES = 4
QN = 256
STRIP = 192
CHUNKS = 3
CW = HD // CHUNKS
LEAD = 3
LAG = 2
MERGE_LAG = 2
FIRST_OWN = 5
NONE = -1e30
FLOOR = -(2.0**96)
RATE = math.log2(math.e) / math.sqrt(HEAD)
TWICE = 1.0 / RATE
MESH = pl.DeviceIdType.MESH
NT = (((1,), (1,)), ((), ()))
TN = (((0,), (0,)), ((), ()))


def dot(a, b, dims):
    return lax.dot_general(a, b, dims, preferred_element_type=jnp.float32)


def kernel(
    owner_ref, slot_ref, span_ref, q_hbm, k_hbm, v_hbm, cache_hbm, out_ref,
    land, q_own, q_far, kv_own, kv_up, kv_dn, strip_out, strip_in, select, mask,
    bias_own, bias_out, bias_far, part_out, part_in, far_sum, far_stat, own_sum, own_stat,
    cache_sem, q_sem, kv_sem, own_ss, own_rs, fwd_ss, fwd_rs, qs, qr, ps, pr,
    bias_ss, bias_rs, row_ss, row_rs, col_ss, col_rs,
):
    clip = lax.axis_index("clip")
    sy = lax.axis_index("sy")
    sx = lax.axis_index("sx")
    rows_n = lax.axis_size("sy")
    cols_n = lax.axis_size("sx")
    x = clip // 2
    yh = clip % 2
    x_next = (lax.rem(clip + 2, 8), sy, sx)
    x_prev = (lax.rem(clip + 6, 8), sy, sx)
    across = (clip + 1 - 2 * yh, sy, sx)
    row_next = (clip, lax.rem(sy + 1, rows_n), sx)
    row_prev = (clip, lax.rem(sy + rows_n - 1, rows_n), sx)
    col_next = (clip, sy, lax.rem(sx + 1, cols_n))
    col_prev = (clip, sy, lax.rem(sx + cols_n - 1, cols_n))

    def lanes(h, width=HEAD):
        return pl.ds(pl.multiple_of(h * width, HEAD), width)

    def cache_copy(h):
        return pltpu.make_async_copy(cache_hbm.at[:, :, :, lanes(h)], land.at[h, 0], cache_sem.at[h])

    def q_copy(h):
        return pltpu.make_async_copy(q_hbm.at[:, lanes(h)], q_own.at[h], q_sem.at[h])

    k_copy = pltpu.make_async_copy(k_hbm, kv_own.at[0], kv_sem.at[0])
    v_copy = pltpu.make_async_copy(v_hbm, kv_own.at[1], kv_sem.at[1])

    def remote(src, dst, ss, rs, device):
        return pltpu.make_async_remote_copy(
            src_ref=src, dst_ref=dst, send_sem=ss, recv_sem=rs, device_id=device, device_id_type=MESH
        )

    def own_send(h, way):
        return remote(
            land.at[h, 0], land.at[h, 1 + way], own_ss.at[way, h], own_rs.at[way, h], (x_next, x_prev)[way]
        )

    def forward(h, way):
        half = pl.ds(2 * way, 2)
        return remote(
            land.at[h, 1 + way, half], land.at[h, 3, half], fwd_ss.at[way, h], fwd_rs.at[way, h],
            (x_next, x_prev)[way],
        )

    def q_send(h):
        return remote(q_own.at[h], q_far.at[h], qs.at[h], qr.at[h], across)

    def part_send(h):
        return remote(part_out.at[h], part_in.at[h], ps.at[h], pr.at[h], across)

    bias_send = remote(bias_out, bias_far, bias_ss, bias_rs, across)

    def row_send(c, way):
        rows = pl.ds(32 * (1 - way), 32)
        return remote(
            kv_own.at[:, :, rows, lanes(c, CW)], (kv_up, kv_dn)[way].at[c], row_ss.at[way, c], row_rs.at[way, c],
            (row_next, row_prev)[way],
        )

    def col_send(c, way):
        return remote(
            strip_out.at[way, c], strip_in.at[way, c], col_ss.at[way, c], col_rs.at[way, c],
            (col_next, col_prev)[way],
        )

    row_has = (sy > 0, sy < rows_n - 1)
    row_to = (sy < rows_n - 1, sy > 0)
    col_has = (sx > 0, sx < cols_n - 1)
    col_to = (sx < cols_n - 1, sx > 0)

    barrier = pltpu.get_barrier_semaphore()

    def greet(device):
        pl.semaphore_signal(barrier, inc=1, device_id=device, device_id_type=MESH)

    for device in (x_next, x_prev, across):
        greet(device)
    for way, device in ((0, row_next), (1, row_prev)):
        pl.when(row_to[way])(functools.partial(greet, device))
    for way, device in ((0, col_next), (1, col_prev)):
        pl.when(col_to[way])(functools.partial(greet, device))

    def start_local(h, carry):
        cache_copy(h).start()
        q_copy(h).start()
        return carry

    lax.fori_loop(0, LEAD, start_local, 0)
    k_copy.start()
    v_copy.start()
    lax.fori_loop(LEAD, HEADS, start_local, 0)

    place = lax.broadcasted_iota(jnp.int32, (16, QN), 0)
    source = place >> 2
    step = jnp.where(source == 0, 0, jnp.where(source == 1, 3, jnp.where(source == 2, 1, 2)))
    base = ((x + step) & 3) * (2 * SLOTS) + (place & 3)
    for ref, half in ((bias_own, yh), (bias_out, 1 - yh)):
        target = base + half * SLOTS
        count = jnp.zeros((16, QN), jnp.int32)
        for j in range(CTX):
            listed = owner_ref[j] * SLOTS + slot_ref[j]
            listed = jnp.where(j // BPC < span_ref[0], listed, -1)
            count = count + jnp.where(target == listed, 1, 0)
        ref[...] = jnp.where(count == 0, NONE, jnp.where(count == 1, 0.0, TWICE)).astype(jnp.float32)

    neighbours = [jnp.where(has, 1, 0) for has in row_has + col_has]
    pl.semaphore_wait(barrier, 3 + sum(neighbours))
    for h in range(LEAD):
        cache_copy(h).wait()
        own_send(h, 0).start()
        own_send(h, 1).start()
        q_copy(h).wait()
        q_send(h).start()
        if h == 0:
            bias_send.start()
    k_copy.wait()
    v_copy.wait()
    for c in range(CHUNKS):
        for way in range(2):
            pl.when(row_to[way])(row_send(c, way).start)

    def fill_edges_and_select():
        for way, ref in ((0, kv_up), (1, kv_dn)):

            @pl.when(jnp.logical_not(row_has[way]))
            def _():
                ref[...] = jnp.zeros_like(ref)

        for way in range(2):

            @pl.when(jnp.logical_not(col_has[way]))
            def _():
                strip_in[way] = jnp.zeros(strip_in.shape[1:], strip_in.dtype)

        strip_row = lax.broadcasted_iota(jnp.int32, (STRIP, 512), 0)
        from_row = lax.broadcasted_iota(jnp.int32, (STRIP, 512), 1)
        frame = (strip_row >> 4) & 3
        height = strip_row & 15
        for way in range(2):
            column = (strip_row >> 6) + (5 if way == 0 else 0)
            wanted = jnp.where(
                height < 4,
                256 + frame * 32 + height * 8,
                jnp.where(height < 12, frame * 64 + (height - 4) * 8, 384 + frame * 32 + (height - 12) * 8),
            )
            select[way] = jnp.where(wanted + column == from_row, 1.0, 0.0).astype(jnp.bfloat16)

    def mask_part(first, count, row_col):
        r = lax.broadcasted_iota(jnp.int32, (count, QN), 0)
        query = lax.broadcasted_iota(jnp.int32, (count, QN), 1)
        row, col = row_col(r)
        down = row - ((query >> 3) & 7)
        right = col - (query & 7)
        row_at = row + sy * 8
        col_at = col + sx * 8
        near = (down <= REACH) & (down >= -REACH) & (right <= REACH) & (right >= -REACH)
        inside = (row_at >= 0) & (row_at < rows_n * 8) & (col_at >= 0) & (col_at < cols_n * 8)
        mask[first : first + count, :] = jnp.where(near & inside, 0.0, NONE).astype(jnp.float32)

    def make_mask():
        mask_part(0, 256, lambda r: ((r >> 3) & 7, r & 7))
        mask_part(256, 128, lambda r: (((r >> 3) & 3) - 4, r & 7))
        mask_part(384, 128, lambda r: (((r >> 3) & 3) + 8, r & 7))
        mask_part(512, STRIP, lambda r: ((r & 15) - 4, (r >> 6) - 3))
        mask_part(512 + STRIP, STRIP, lambda r: ((r & 15) - 4, (r >> 6) + 8))

    def ring_scores(h, query, bias, blocks):
        scores, highest = [], jnp.full((1, QN), FLOOR, jnp.float32)
        for r in blocks:
            s = dot(land[h, r, :, 0].reshape(QN, HEAD), query, NT)
            for b in range(4):
                top = jnp.max(s[b * BLK : (b + 1) * BLK], axis=0, keepdims=True)
                highest = jnp.maximum(highest, top + bias[4 * r + b : 4 * r + b + 1])
            scores.append(s)
        return scores, highest

    def ring_sums(h, scores, highest, bias, blocks, total, mixed):
        for r, s in zip(blocks, scores):
            shift = [highest - bias[4 * r + b : 4 * r + b + 1] for b in range(4)]
            p = jnp.concatenate([jnp.exp2((s[b * BLK : (b + 1) * BLK] - shift[b]) * RATE) for b in range(4)], 0)
            total = total + jnp.sum(p, axis=0, keepdims=True)
            mixed = mixed + dot(land[h, r, :, 1].reshape(QN, HEAD), p.astype(jnp.bfloat16), TN)
        return total, mixed

    def no_sum():
        return jnp.zeros((1, QN), jnp.float32), jnp.zeros((HEAD, QN), jnp.float32)

    def far_early(h):
        bias = bias_far[...]
        scores, highest = ring_scores(h, q_far[h], bias, (0, 1, 2))
        total, mixed = ring_sums(h, scores, highest, bias, (0, 1, 2), *no_sum())
        at = lax.rem(h, LAG + 1)
        far_sum[at] = mixed
        far_stat[at, 0:1] = highest
        far_stat[at, 1:2] = total

    def far_late(h):
        bias = bias_far[...]
        at = lax.rem(h, LAG + 1)
        early_highest, early_total = far_stat[at, 0:1], far_stat[at, 1:2]
        scores, highest = ring_scores(h, q_far[h], bias, (3,))
        highest = jnp.maximum(highest, early_highest).astype(jnp.bfloat16).astype(jnp.float32)
        early = jnp.exp2((early_highest - highest) * RATE)
        total, mixed = ring_sums(h, scores, highest, bias, (3,), early_total * early, far_sum[at] * early)
        coarse = total.astype(jnp.bfloat16).astype(jnp.float32)
        row = lax.broadcasted_iota(jnp.int32, (16, QN), 0)
        stats = jnp.where(row == 0, highest, jnp.where(row == 1, coarse, total - coarse))
        part_out[h, :HEAD] = mixed.astype(jnp.bfloat16)
        part_out[h, HEAD:] = stats.astype(jnp.bfloat16)

    def attend_own(h):
        query = q_own[h]
        bias = bias_own[...]
        c = h // (HEADS // CHUNKS)
        here = lanes(h - c * (HEADS // CHUNKS))

        def pieces(kv):
            own = kv_own[kv, :, :, lanes(h)].reshape(QN, HEAD)
            up = kv_up[c, kv, :, :, here].reshape(128, HEAD)
            dn = kv_dn[c, kv, :, :, here].reshape(128, HEAD)
            left = strip_in[0, c, kv, :, here]
            right = strip_in[1, c, kv, :, here]
            return own, jnp.concatenate([up, dn], 0), jnp.concatenate([left, right], 0)

        blocks = (0, 1, 2, 3)
        scores, highest = ring_scores(h, query, bias, blocks)
        near, first = [], 0
        for piece in pieces(0):
            s = dot(piece, query, NT) + mask[first : first + piece.shape[0], :]
            first += piece.shape[0]
            highest = jnp.maximum(highest, jnp.max(s, axis=0, keepdims=True))
            near.append(s)
        total, mixed = ring_sums(h, scores, highest, bias, blocks, *no_sum())
        for piece, s in zip(pieces(1), near):
            p = jnp.exp2((s - highest) * RATE)
            total = total + jnp.sum(p, axis=0, keepdims=True)
            mixed = mixed + dot(piece, p.astype(jnp.bfloat16), TN)
        own_sum[h] = mixed
        own_stat[h, 0:1] = highest
        own_stat[h, 1:2] = total

    def merge(h):
        part_send(h).wait_recv()
        stats = part_in[h, HEAD:].astype(jnp.float32)
        far_highest, far_total = stats[0:1], stats[1:2] + stats[2:3]
        highest, total = own_stat[h, 0:1], own_stat[h, 1:2]
        top = jnp.maximum(highest, far_highest)
        here_scale = jnp.exp2((highest - top) * RATE)
        far_scale = jnp.exp2((far_highest - top) * RATE)
        inverse = 1.0 / (total * here_scale + far_total * far_scale)
        result = own_sum[h] * (here_scale * inverse) + part_in[h, :HEAD].astype(jnp.float32) * (far_scale * inverse)
        out_ref[:, lanes(h)] = result.T.astype(jnp.bfloat16)

    def make_strips(c):
        for way in range(2):
            pl.when(row_has[way])(row_send(c, way).wait_recv)
        for kv in range(2):
            tile = kv_own[kv, :, :, lanes(c, CW)].reshape(QN, CW)
            halo = jnp.concatenate([kv_up[c, kv].reshape(128, CW), kv_dn[c, kv].reshape(128, CW)], 0)
            for way in range(2):
                packed = jnp.dot(select[way, :, :QN], tile, preferred_element_type=jnp.float32)
                packed = packed + jnp.dot(select[way, :, QN:], halo, preferred_element_type=jnp.float32)
                strip_out[way, c, kv] = packed.astype(jnp.bfloat16)
        for way in range(2):
            pl.when(col_to[way])(col_send(c, way).start)

    def ring_step(h, carry):
        @pl.when(h < HEADS)
        def _():
            for way in range(2):
                own_send(h, way).wait_recv()
                forward(h, way).start()

        @pl.when(h + LEAD < HEADS)
        def _():
            cache_copy(h + LEAD).wait()
            own_send(h + LEAD, 0).start()
            own_send(h + LEAD, 1).start()
            q_copy(h + LEAD).wait()
            q_send(h + LEAD).start()

        pl.when(h == 0)(fill_edges_and_select)
        pl.when(h == 1)(make_mask)

        @pl.when((h >= 2) & (h < 2 + CHUNKS))
        def _():
            make_strips(h - 2)

        @pl.when(h >= LAG)
        def _():
            for way in range(2):
                forward(h - LAG, way).wait_recv()
            far_late(h - LAG)
            part_send(h - LAG).start()

        @pl.when(h < HEADS)
        def _():
            q_send(h).wait_recv()
            pl.when(h == 0)(bias_send.wait_recv)
            far_early(h)

        def merge_step(i, carry):
            merge(i)
            return carry

        def own_step(i, carry):
            @pl.when(lax.rem(i, HEADS // CHUNKS) == 0)
            def _():
                for way in range(2):
                    pl.when(col_has[way])(col_send(i // (HEADS // CHUNKS), way).wait_recv)

            attend_own(i)
            return carry

        lax.fori_loop(own_done(h - MERGE_LAG), own_done(h - MERGE_LAG + 1), merge_step, 0)
        lax.fori_loop(own_done(h), own_done(h + 1), own_step, 0)
        return carry

    def own_done(step):
        return jnp.clip(2 * (step - FIRST_OWN), 0, jnp.maximum(step - LAG, 0))

    steps = HEADS + LAG
    lax.fori_loop(0, steps, ring_step, 0)
    for h in range(min(2 * (steps - MERGE_LAG - FIRST_OWN), HEADS - MERGE_LAG), HEADS):
        merge(h)

    def finish(h, carry):
        for way in range(2):
            own_send(h, way).wait_send()
            forward(h, way).wait_send()
        q_send(h).wait_send()
        part_send(h).wait_send()
        return carry

    lax.fori_loop(0, HEADS, finish, 0)
    bias_send.wait_send()
    for c in range(CHUNKS):
        for way in range(2):
            pl.when(row_to[way])(row_send(c, way).wait_send)
            pl.when(col_to[way])(col_send(c, way).wait_send)


def per_device(queries, keys, values, cache, ctx_owner, ctx_slot, span_count):
    bf16, f32, dma = jnp.bfloat16, jnp.float32, pltpu.SemaphoreType.DMA
    smem = pl.BlockSpec(memory_space=pltpu.SMEM)
    anywhere = pl.BlockSpec(memory_space=pl.ANY)
    attended = pl.pallas_call(
        kernel,
        out_shape=pltpu.VMEM((QN, HD), bf16),
        in_specs=[smem] * 3 + [anywhere] * 4,
        out_specs=pl.BlockSpec(memory_space=pltpu.VMEM),
        scratch_shapes=[
            pltpu.VMEM((HEADS, 4, SLOTS, 2, BLK, HEAD), bf16),
            pltpu.VMEM((HEADS, QN, HEAD), bf16),
            pltpu.VMEM((HEADS, QN, HEAD), bf16),
            pltpu.VMEM((2, FRAMES, 64, HD), bf16),
            pltpu.VMEM((CHUNKS, 2, FRAMES, 32, CW), bf16),
            pltpu.VMEM((CHUNKS, 2, FRAMES, 32, CW), bf16),
            pltpu.VMEM((2, CHUNKS, 2, STRIP, CW), bf16),
            pltpu.VMEM((2, CHUNKS, 2, STRIP, CW), bf16),
            pltpu.VMEM((2, STRIP, 512), bf16),
            pltpu.VMEM((512 + 2 * STRIP, QN), f32),
            pltpu.VMEM((16, QN), f32),
            pltpu.VMEM((16, QN), f32),
            pltpu.VMEM((16, QN), f32),
            pltpu.VMEM((HEADS, HEAD + 16, QN), bf16),
            pltpu.VMEM((HEADS, HEAD + 16, QN), bf16),
            pltpu.VMEM((LAG + 1, HEAD, QN), f32),
            pltpu.VMEM((LAG + 1, 8, QN), f32),
            pltpu.VMEM((HEADS, HEAD, QN), f32),
            pltpu.VMEM((HEADS, 8, QN), f32),
            dma((HEADS,)), dma((HEADS,)), dma((2,)),
            dma((2, HEADS)), dma((2, HEADS)), dma((2, HEADS)), dma((2, HEADS)),
            dma((HEADS,)), dma((HEADS,)), dma((HEADS,)), dma((HEADS,)),
            dma, dma,
            dma((2, CHUNKS)), dma((2, CHUNKS)), dma((2, CHUNKS)), dma((2, CHUNKS)),
        ],
        compiler_params=pltpu.CompilerParams(
            collective_id=0, has_side_effects=True, vmem_limit_bytes=60 * 2**20
        ),
        cost_estimate=pl.CostEstimate(flops=4 * QN * 2944 * HD, bytes_accessed=6 * 2**20, transcendentals=QN * 2944 * HEADS),
        name="span_attention",
    )(
        ctx_owner.reshape(-1),
        ctx_slot.reshape(-1),
        span_count.reshape(-1),
        queries.reshape(QN, HD),
        keys.reshape(FRAMES, 64, HD),
        values.reshape(FRAMES, 64, HD),
        cache.reshape(SLOTS, 2, BLK, HD),
    )
    return attended.reshape(queries.shape)


def solution(mesh):
    placed = (
        P("clip", None, "sy", "sx", None),
        P("clip", None, "sy", "sx", None),
        P("clip", None, "sy", "sx", None),
        P("clip", "sy", "sx", None, None, None),
        P("clip", "sy", "sx", None),
        P("clip", "sy", "sx", None),
        P("clip"),
    )
    return jax.shard_map(
        per_device,
        mesh=mesh,
        in_specs=placed,
        out_specs=P("clip", None, "sy", "sx", None),
        check_vma=False,
    )
```

```python
import functools
import math

import jax
import jax.numpy as jnp
from jax import lax
from jax.experimental import pallas as pl
from jax.experimental.pallas import tpu as pltpu
from jax.sharding import PartitionSpec as P

HEAD = 128
HEADS = 12
HD = HEAD * HEADS
REACH = 3
BLK = 64
BPC = 2
CTX = 8
SLOTS = 4
FRAMES = 4
QN = 256
STRIP = 192
CHUNKS = 3
CW = HD // CHUNKS
LEAD = 3
EARLY = 8
LAST_LEAD = 2
LAG = 2
MERGE_LAG = 2
FIRST_OWN = 5
NONE = -1e30
FLOOR = -(2.0**96)
RATE = math.log2(math.e) / math.sqrt(HEAD)
TWICE = 1.0 / RATE
MESH = pl.DeviceIdType.MESH
NT = (((1,), (1,)), ((), ()))
TN = (((0,), (0,)), ((), ()))


def dot(a, b, dims):
    return lax.dot_general(a, b, dims, preferred_element_type=jnp.float32)


def kernel(
    owner_ref, slot_ref, span_ref, q_hbm, k_hbm, v_hbm, cache_hbm, out_ref,
    land, q_own, q_far, kv_own, kv_up, kv_dn, strip_out, strip_in, select, mask,
    bias_own, bias_out, bias_far, part_out, part_in, far_sum, far_stat, own_sum, own_stat,
    cache_sem, q_sem, kv_sem, own_ss, own_rs, fwd_ss, fwd_rs, qs, qr, ps, pr,
    bias_ss, bias_rs, row_ss, row_rs, col_ss, col_rs,
):
    clip = lax.axis_index("clip")
    sy = lax.axis_index("sy")
    sx = lax.axis_index("sx")
    rows_n = lax.axis_size("sy")
    cols_n = lax.axis_size("sx")
    x = clip // 2
    yh = clip % 2
    x_next = (lax.rem(clip + 2, 8), sy, sx)
    x_prev = (lax.rem(clip + 6, 8), sy, sx)
    across = (clip + 1 - 2 * yh, sy, sx)
    row_next = (clip, lax.rem(sy + 1, rows_n), sx)
    row_prev = (clip, lax.rem(sy + rows_n - 1, rows_n), sx)
    col_next = (clip, sy, lax.rem(sx + 1, cols_n))
    col_prev = (clip, sy, lax.rem(sx + cols_n - 1, cols_n))

    def lanes(h, width=HEAD):
        return pl.ds(pl.multiple_of(h * width, HEAD), width)

    def cache_copy(h):
        return pltpu.make_async_copy(cache_hbm.at[:, :, :, lanes(h)], land.at[h, 0], cache_sem.at[h])

    def q_copy(h):
        return pltpu.make_async_copy(q_hbm.at[:, lanes(h)], q_own.at[h], q_sem.at[h])

    k_copy = pltpu.make_async_copy(k_hbm, kv_own.at[0], kv_sem.at[0])
    v_copy = pltpu.make_async_copy(v_hbm, kv_own.at[1], kv_sem.at[1])

    def remote(src, dst, ss, rs, device):
        return pltpu.make_async_remote_copy(
            src_ref=src, dst_ref=dst, send_sem=ss, recv_sem=rs, device_id=device, device_id_type=MESH
        )

    def own_send(h, way):
        return remote(
            land.at[h, 0], land.at[h, 1 + way], own_ss.at[way, h], own_rs.at[way, h], (x_next, x_prev)[way]
        )

    def own_first(h, way):
        return remote(
            cache_hbm.at[:, :, :, lanes(h)], land.at[h, 1 + way], own_ss.at[way, h], own_rs.at[way, h],
            (x_next, x_prev)[way],
        )

    def forward(h, way):
        half = pl.ds(2 * way, 2)
        return remote(
            land.at[h, 1 + way, half], land.at[h, 3, half], fwd_ss.at[way, h], fwd_rs.at[way, h],
            (x_next, x_prev)[way],
        )

    def q_send(h):
        return remote(q_own.at[h], q_far.at[h], qs.at[h], qr.at[h], across)

    def part_send(h):
        return remote(part_out.at[h], part_in.at[h], ps.at[h], pr.at[h], across)

    bias_send = remote(bias_out, bias_far, bias_ss, bias_rs, across)

    def row_send(c, way):
        rows = pl.ds(32 * (1 - way), 32)
        return remote(
            kv_own.at[:, :, rows, lanes(c, CW)], (kv_up, kv_dn)[way].at[c], row_ss.at[way, c], row_rs.at[way, c],
            (row_next, row_prev)[way],
        )

    def col_send(c, way):
        return remote(
            strip_out.at[way, c], strip_in.at[way, c], col_ss.at[way, c], col_rs.at[way, c],
            (col_next, col_prev)[way],
        )

    row_has = (sy > 0, sy < rows_n - 1)
    row_to = (sy < rows_n - 1, sy > 0)
    col_has = (sx > 0, sx < cols_n - 1)
    col_to = (sx < cols_n - 1, sx > 0)

    barrier = pltpu.get_barrier_semaphore()

    def greet(device):
        pl.semaphore_signal(barrier, inc=1, device_id=device, device_id_type=MESH)

    for device in (x_next, x_prev, across):
        greet(device)
    for way, device in ((0, row_next), (1, row_prev)):
        pl.when(row_to[way])(functools.partial(greet, device))
    for way, device in ((0, col_next), (1, col_prev)):
        pl.when(col_to[way])(functools.partial(greet, device))

    def start_local(h, carry):
        cache_copy(h).start()
        q_copy(h).start()
        return carry

    lax.fori_loop(0, LEAD, start_local, 0)
    k_copy.start()
    v_copy.start()
    lax.fori_loop(LEAD, HEADS, start_local, 0)

    neighbours = [jnp.where(has, 1, 0) for has in row_has + col_has]
    pl.semaphore_wait(barrier, 3 + sum(neighbours))
    for h in range(LEAD):
        own_first(h, 0).start()
        own_first(h, 1).start()
    for h in range(LEAD):
        q_copy(h).wait()
        q_send(h).start()

    place = lax.broadcasted_iota(jnp.int32, (16, QN), 0)
    source = place >> 2
    step = jnp.where(source == 0, 0, jnp.where(source == 1, 3, jnp.where(source == 2, 1, 2)))
    base = ((x + step) & 3) * (2 * SLOTS) + (place & 3)
    for ref, half in ((bias_own, yh), (bias_out, 1 - yh)):
        target = base + half * SLOTS
        count = jnp.zeros((16, QN), jnp.int32)
        for j in range(CTX):
            listed = owner_ref[j] * SLOTS + slot_ref[j]
            listed = jnp.where(j // BPC < span_ref[0], listed, -1)
            count = count + jnp.where(target == listed, 1, 0)
        ref[...] = jnp.where(count == 0, NONE, jnp.where(count == 1, 0.0, TWICE)).astype(jnp.float32)

    bias_send.start()
    for h in range(LEAD):
        cache_copy(h).wait()
    k_copy.wait()
    v_copy.wait()
    for c in range(CHUNKS):
        for way in range(2):
            pl.when(row_to[way])(row_send(c, way).start)

    def fill_edges_and_select():
        for way, ref in ((0, kv_up), (1, kv_dn)):

            @pl.when(jnp.logical_not(row_has[way]))
            def _():
                ref[...] = jnp.zeros_like(ref)

        for way in range(2):

            @pl.when(jnp.logical_not(col_has[way]))
            def _():
                strip_in[way] = jnp.zeros(strip_in.shape[1:], strip_in.dtype)

        strip_row = lax.broadcasted_iota(jnp.int32, (STRIP, 512), 0)
        from_row = lax.broadcasted_iota(jnp.int32, (STRIP, 512), 1)
        frame = (strip_row >> 4) & 3
        height = strip_row & 15
        for way in range(2):
            column = (strip_row >> 6) + (5 if way == 0 else 0)
            wanted = jnp.where(
                height < 4,
                256 + frame * 32 + height * 8,
                jnp.where(height < 12, frame * 64 + (height - 4) * 8, 384 + frame * 32 + (height - 12) * 8),
            )
            select[way] = jnp.where(wanted + column == from_row, 1.0, 0.0).astype(jnp.bfloat16)

    def mask_part(first, count, row_col):
        r = lax.broadcasted_iota(jnp.int32, (count, QN), 0)
        query = lax.broadcasted_iota(jnp.int32, (count, QN), 1)
        row, col = row_col(r)
        down = row - ((query >> 3) & 7)
        right = col - (query & 7)
        row_at = row + sy * 8
        col_at = col + sx * 8
        near = (down <= REACH) & (down >= -REACH) & (right <= REACH) & (right >= -REACH)
        inside = (row_at >= 0) & (row_at < rows_n * 8) & (col_at >= 0) & (col_at < cols_n * 8)
        mask[first : first + count, :] = jnp.where(near & inside, 0.0, NONE).astype(jnp.float32)

    def make_mask():
        mask_part(0, 256, lambda r: ((r >> 3) & 7, r & 7))
        mask_part(256, 128, lambda r: (((r >> 3) & 3) - 4, r & 7))
        mask_part(384, 128, lambda r: (((r >> 3) & 3) + 8, r & 7))
        mask_part(512, STRIP, lambda r: ((r & 15) - 4, (r >> 6) - 3))
        mask_part(512 + STRIP, STRIP, lambda r: ((r & 15) - 4, (r >> 6) + 8))

    def ring_scores(h, query, bias, blocks):
        scores, highest = [], jnp.full((1, QN), FLOOR, jnp.float32)
        for r in blocks:
            s = dot(land[h, r, :, 0].reshape(QN, HEAD), query, NT)
            for b in range(4):
                top = jnp.max(s[b * BLK : (b + 1) * BLK], axis=0, keepdims=True)
                highest = jnp.maximum(highest, top + bias[4 * r + b : 4 * r + b + 1])
            scores.append(s)
        return scores, highest

    def ring_sums(h, scores, highest, bias, blocks, total, mixed):
        for r, s in zip(blocks, scores):
            shift = [highest - bias[4 * r + b : 4 * r + b + 1] for b in range(4)]
            p = jnp.concatenate([jnp.exp2((s[b * BLK : (b + 1) * BLK] - shift[b]) * RATE) for b in range(4)], 0)
            total = total + jnp.sum(p, axis=0, keepdims=True)
            mixed = mixed + dot(land[h, r, :, 1].reshape(QN, HEAD), p.astype(jnp.bfloat16), TN)
        return total, mixed

    def no_sum():
        return jnp.zeros((1, QN), jnp.float32), jnp.zeros((HEAD, QN), jnp.float32)

    def far_early(h):
        bias = bias_far[...]
        scores, highest = ring_scores(h, q_far[h], bias, (0, 1, 2))
        total, mixed = ring_sums(h, scores, highest, bias, (0, 1, 2), *no_sum())
        at = lax.rem(h, LAG + 1)
        far_sum[at] = mixed
        far_stat[at, 0:1] = highest
        far_stat[at, 1:2] = total

    def far_late(h):
        bias = bias_far[...]
        at = lax.rem(h, LAG + 1)
        early_highest, early_total = far_stat[at, 0:1], far_stat[at, 1:2]
        scores, highest = ring_scores(h, q_far[h], bias, (3,))
        highest = jnp.maximum(highest, early_highest).astype(jnp.bfloat16).astype(jnp.float32)
        early = jnp.exp2((early_highest - highest) * RATE)
        total, mixed = ring_sums(h, scores, highest, bias, (3,), early_total * early, far_sum[at] * early)
        coarse = total.astype(jnp.bfloat16).astype(jnp.float32)
        row = lax.broadcasted_iota(jnp.int32, (16, QN), 0)
        stats = jnp.where(row == 0, highest, jnp.where(row == 1, coarse, total - coarse))
        part_out[h, :HEAD] = mixed.astype(jnp.bfloat16)
        part_out[h, HEAD:] = stats.astype(jnp.bfloat16)

    def attend_own(h):
        query = q_own[h]
        bias = bias_own[...]
        c = h // (HEADS // CHUNKS)
        here = lanes(h - c * (HEADS // CHUNKS))

        def pieces(kv):
            own = kv_own[kv, :, :, lanes(h)].reshape(QN, HEAD)
            up = kv_up[c, kv, :, :, here].reshape(128, HEAD)
            dn = kv_dn[c, kv, :, :, here].reshape(128, HEAD)
            left = strip_in[0, c, kv, :, here]
            right = strip_in[1, c, kv, :, here]
            return own, jnp.concatenate([up, dn], 0), jnp.concatenate([left, right], 0)

        blocks = (0, 1, 2, 3)
        scores, highest = ring_scores(h, query, bias, blocks)
        near, first = [], 0
        for piece in pieces(0):
            s = dot(piece, query, NT) + mask[first : first + piece.shape[0], :]
            first += piece.shape[0]
            highest = jnp.maximum(highest, jnp.max(s, axis=0, keepdims=True))
            near.append(s)
        total, mixed = ring_sums(h, scores, highest, bias, blocks, *no_sum())
        for piece, s in zip(pieces(1), near):
            p = jnp.exp2((s - highest) * RATE)
            total = total + jnp.sum(p, axis=0, keepdims=True)
            mixed = mixed + dot(piece, p.astype(jnp.bfloat16), TN)
        own_sum[h] = mixed
        own_stat[h, 0:1] = highest
        own_stat[h, 1:2] = total

    def merge(h):
        part_send(h).wait_recv()
        stats = part_in[h, HEAD:].astype(jnp.float32)
        far_highest, far_total = stats[0:1], stats[1:2] + stats[2:3]
        highest, total = own_stat[h, 0:1], own_stat[h, 1:2]
        top = jnp.maximum(highest, far_highest)
        here_scale = jnp.exp2((highest - top) * RATE)
        far_scale = jnp.exp2((far_highest - top) * RATE)
        inverse = 1.0 / (total * here_scale + far_total * far_scale)
        result = own_sum[h] * (here_scale * inverse) + part_in[h, :HEAD].astype(jnp.float32) * (far_scale * inverse)
        out_ref[:, lanes(h)] = result.T.astype(jnp.bfloat16)

    def make_strips(c):
        for way in range(2):
            pl.when(row_has[way])(row_send(c, way).wait_recv)
        for kv in range(2):
            tile = kv_own[kv, :, :, lanes(c, CW)].reshape(QN, CW)
            halo = jnp.concatenate([kv_up[c, kv].reshape(128, CW), kv_dn[c, kv].reshape(128, CW)], 0)
            for way in range(2):
                packed = jnp.dot(select[way, :, :QN], tile, preferred_element_type=jnp.float32)
                packed = packed + jnp.dot(select[way, :, QN:], halo, preferred_element_type=jnp.float32)
                strip_out[way, c, kv] = packed.astype(jnp.bfloat16)
        for way in range(2):
            pl.when(col_to[way])(col_send(c, way).start)

    def ring_step(h, carry):
        @pl.when(h < HEADS)
        def _():
            for way in range(2):
                own_send(h, way).wait_recv()
                forward(h, way).start()

        def send_step(i, carry):
            cache_copy(i).wait()
            own_send(i, 0).start()
            own_send(i, 1).start()
            return carry

        lax.fori_loop(sent(h), sent(h + 1), send_step, 0)

        @pl.when(h + LEAD < HEADS)
        def _():
            q_copy(h + LEAD).wait()
            q_send(h + LEAD).start()

        pl.when(h == 0)(fill_edges_and_select)
        pl.when(h == 1)(make_mask)

        @pl.when((h >= 2) & (h < 2 + CHUNKS))
        def _():
            make_strips(h - 2)

        @pl.when(h >= LAG)
        def _():
            for way in range(2):
                forward(h - LAG, way).wait_recv()
            far_late(h - LAG)
            part_send(h - LAG).start()

        @pl.when(h < HEADS)
        def _():
            q_send(h).wait_recv()
            pl.when(h == 0)(bias_send.wait_recv)
            far_early(h)

        def merge_step(i, carry):
            merge(i)
            return carry

        def own_step(i, carry):
            @pl.when(lax.rem(i, HEADS // CHUNKS) == 0)
            def _():
                for way in range(2):
                    pl.when(col_has[way])(col_send(i // (HEADS // CHUNKS), way).wait_recv)

            attend_own(i)
            return carry

        lax.fori_loop(own_done(h - MERGE_LAG), own_done(h - MERGE_LAG + 1), merge_step, 0)
        lax.fori_loop(own_done(h), own_done(h + 1), own_step, 0)
        return carry

    def sent(step):
        return jnp.minimum(jnp.minimum(step + LEAD, jnp.maximum(EARLY, step + LAST_LEAD)), HEADS)

    def own_done(step):
        caught_up = jnp.clip(2 * (step - FIRST_OWN), 0, jnp.maximum(step - LAG - 1, 0))
        return jnp.where(step >= steps, HEADS, caught_up)

    steps = HEADS + LAG
    lax.fori_loop(0, steps, ring_step, 0)
    for h in range(HEADS - MERGE_LAG - 1, HEADS - 1):
        merge(h)

    def finish(h, carry):
        for way in range(2):
            own_send(h, way).wait_send()
            forward(h, way).wait_send()
        q_send(h).wait_send()
        part_send(h).wait_send()
        return carry

    lax.fori_loop(0, HEADS, finish, 0)
    bias_send.wait_send()
    for c in range(CHUNKS):
        for way in range(2):
            pl.when(row_to[way])(row_send(c, way).wait_send)
            pl.when(col_to[way])(col_send(c, way).wait_send)
    merge(HEADS - 1)


def per_device(queries, keys, values, cache, ctx_owner, ctx_slot, span_count):
    bf16, f32, dma = jnp.bfloat16, jnp.float32, pltpu.SemaphoreType.DMA
    smem = pl.BlockSpec(memory_space=pltpu.SMEM)
    anywhere = pl.BlockSpec(memory_space=pl.ANY)
    attended = pl.pallas_call(
        kernel,
        out_shape=pltpu.VMEM((QN, HD), bf16),
        in_specs=[smem] * 3 + [anywhere] * 4,
        out_specs=pl.BlockSpec(memory_space=pltpu.VMEM),
        scratch_shapes=[
            pltpu.VMEM((HEADS, 4, SLOTS, 2, BLK, HEAD), bf16),
            pltpu.VMEM((HEADS, QN, HEAD), bf16),
            pltpu.VMEM((HEADS, QN, HEAD), bf16),
            pltpu.VMEM((2, FRAMES, 64, HD), bf16),
            pltpu.VMEM((CHUNKS, 2, FRAMES, 32, CW), bf16),
            pltpu.VMEM((CHUNKS, 2, FRAMES, 32, CW), bf16),
            pltpu.VMEM((2, CHUNKS, 2, STRIP, CW), bf16),
            pltpu.VMEM((2, CHUNKS, 2, STRIP, CW), bf16),
            pltpu.VMEM((2, STRIP, 512), bf16),
            pltpu.VMEM((512 + 2 * STRIP, QN), f32),
            pltpu.VMEM((16, QN), f32),
            pltpu.VMEM((16, QN), f32),
            pltpu.VMEM((16, QN), f32),
            pltpu.VMEM((HEADS, HEAD + 16, QN), bf16),
            pltpu.VMEM((HEADS, HEAD + 16, QN), bf16),
            pltpu.VMEM((LAG + 1, HEAD, QN), f32),
            pltpu.VMEM((LAG + 1, 8, QN), f32),
            pltpu.VMEM((HEADS, HEAD, QN), f32),
            pltpu.VMEM((HEADS, 8, QN), f32),
            dma((HEADS,)), dma((HEADS,)), dma((2,)),
            dma((2, HEADS)), dma((2, HEADS)), dma((2, HEADS)), dma((2, HEADS)),
            dma((HEADS,)), dma((HEADS,)), dma((HEADS,)), dma((HEADS,)),
            dma, dma,
            dma((2, CHUNKS)), dma((2, CHUNKS)), dma((2, CHUNKS)), dma((2, CHUNKS)),
        ],
        compiler_params=pltpu.CompilerParams(
            collective_id=0, has_side_effects=True, vmem_limit_bytes=60 * 2**20
        ),
        cost_estimate=pl.CostEstimate(flops=4 * QN * 2944 * HD, bytes_accessed=6 * 2**20, transcendentals=QN * 2944 * HEADS),
        name="span_attention",
    )(
        ctx_owner.reshape(-1),
        ctx_slot.reshape(-1),
        span_count.reshape(-1),
        queries.reshape(QN, HD),
        keys.reshape(FRAMES, 64, HD),
        values.reshape(FRAMES, 64, HD),
        cache.reshape(SLOTS, 2, BLK, HD),
    )
    return attended.reshape(queries.shape)


def solution(mesh):
    placed = (
        P("clip", None, "sy", "sx", None),
        P("clip", None, "sy", "sx", None),
        P("clip", None, "sy", "sx", None),
        P("clip", "sy", "sx", None, None, None),
        P("clip", "sy", "sx", None),
        P("clip", "sy", "sx", None),
        P("clip"),
    )
    return jax.shard_map(
        per_device,
        mesh=mesh,
        in_specs=placed,
        out_specs=P("clip", None, "sy", "sx", None),
        check_vma=False,
    )
```

```python
import functools
import math

import jax
import jax.numpy as jnp
from jax import lax
from jax.experimental import pallas as pl
from jax.experimental.pallas import tpu as pltpu
from jax.sharding import PartitionSpec as P

HEAD = 128
HEADS = 12
HD = HEAD * HEADS
REACH = 3
BLK = 64
BPC = 2
CTX = 8
SLOTS = 4
FRAMES = 4
QN = 256
STRIP = 192
CHUNKS = 3
CW = HD // CHUNKS
LEAD = 3
EARLY = 8
LAST_LEAD = 2
LAG = 2
MERGE_LAG = 2
FIRST_OWN = 6
NONE = -1e30
FLOOR = -(2.0**96)
RATE = math.log2(math.e) / math.sqrt(HEAD)
TWICE = 1.0 / RATE
MESH = pl.DeviceIdType.MESH
NT = (((1,), (1,)), ((), ()))
TN = (((0,), (0,)), ((), ()))


def dot(a, b, dims):
    return lax.dot_general(a, b, dims, preferred_element_type=jnp.float32)


def kernel(
    owner_ref, slot_ref, span_ref, q_hbm, k_hbm, v_hbm, cache_hbm, out_ref,
    land, q_own, q_far, kv_own, kv_up, kv_dn, strip_out, strip_in, select, mask,
    bias_own, bias_out, bias_far, part_out, part_in, far_sum, far_stat, own_sum, own_stat,
    cache_sem, q_sem, kv_sem, own_ss, own_rs, fwd_ss, fwd_rs, qs, qr, ps, pr,
    bias_ss, bias_rs, row_ss, row_rs, col_ss, col_rs,
):
    clip = lax.axis_index("clip")
    sy = lax.axis_index("sy")
    sx = lax.axis_index("sx")
    rows_n = lax.axis_size("sy")
    cols_n = lax.axis_size("sx")
    x = clip // 2
    yh = clip % 2
    x_next = (lax.rem(clip + 2, 8), sy, sx)
    x_prev = (lax.rem(clip + 6, 8), sy, sx)
    across = (clip + 1 - 2 * yh, sy, sx)
    row_next = (clip, lax.rem(sy + 1, rows_n), sx)
    row_prev = (clip, lax.rem(sy + rows_n - 1, rows_n), sx)
    col_next = (clip, sy, lax.rem(sx + 1, cols_n))
    col_prev = (clip, sy, lax.rem(sx + cols_n - 1, cols_n))

    def lanes(h, width=HEAD):
        return pl.ds(pl.multiple_of(h * width, HEAD), width)

    def cache_copy(h):
        return pltpu.make_async_copy(cache_hbm.at[:, :, :, lanes(h)], land.at[h, 0], cache_sem.at[h])

    def q_copy(h):
        return pltpu.make_async_copy(q_hbm.at[:, lanes(h)], q_own.at[h], q_sem.at[h])

    k_copy = pltpu.make_async_copy(k_hbm, kv_own.at[0], kv_sem.at[0])
    v_copy = pltpu.make_async_copy(v_hbm, kv_own.at[1], kv_sem.at[1])

    def remote(src, dst, ss, rs, device):
        return pltpu.make_async_remote_copy(
            src_ref=src, dst_ref=dst, send_sem=ss, recv_sem=rs, device_id=device, device_id_type=MESH
        )

    def own_send(h, way):
        return remote(
            land.at[h, 0], land.at[h, 1 + way], own_ss.at[way, h], own_rs.at[way, h], (x_next, x_prev)[way]
        )

    def own_first(h, way):
        return remote(
            cache_hbm.at[:, :, :, lanes(h)], land.at[h, 1 + way], own_ss.at[way, h], own_rs.at[way, h],
            (x_next, x_prev)[way],
        )

    def forward(h, way):
        half = pl.ds(2 * way, 2)
        return remote(
            land.at[h, 1 + way, half], land.at[h, 3, half], fwd_ss.at[way, h], fwd_rs.at[way, h],
            (x_next, x_prev)[way],
        )

    def q_send(h):
        return remote(q_own.at[h], q_far.at[h], qs.at[h], qr.at[h], across)

    def part_send(h):
        return remote(part_out.at[h], part_in.at[h], ps.at[h], pr.at[h], across)

    bias_send = remote(bias_out, bias_far, bias_ss, bias_rs, across)

    def row_send(c, way):
        rows = pl.ds(32 * (1 - way), 32)
        return remote(
            kv_own.at[:, :, rows, lanes(c, CW)], (kv_up, kv_dn)[way].at[c], row_ss.at[way, c], row_rs.at[way, c],
            (row_next, row_prev)[way],
        )

    def col_send(c, way):
        return remote(
            strip_out.at[way, c], strip_in.at[way, c], col_ss.at[way, c], col_rs.at[way, c],
            (col_next, col_prev)[way],
        )

    row_has = (sy > 0, sy < rows_n - 1)
    row_to = (sy < rows_n - 1, sy > 0)
    col_has = (sx > 0, sx < cols_n - 1)
    col_to = (sx < cols_n - 1, sx > 0)

    barrier = pltpu.get_barrier_semaphore()

    def greet(device):
        pl.semaphore_signal(barrier, inc=1, device_id=device, device_id_type=MESH)

    for device in (x_next, x_prev, across):
        greet(device)
    for way, device in ((0, row_next), (1, row_prev)):
        pl.when(row_to[way])(functools.partial(greet, device))
    for way, device in ((0, col_next), (1, col_prev)):
        pl.when(col_to[way])(functools.partial(greet, device))

    def start_local(h, carry):
        cache_copy(h).start()
        q_copy(h).start()
        return carry

    lax.fori_loop(0, LEAD, start_local, 0)
    k_copy.start()
    v_copy.start()
    lax.fori_loop(LEAD, HEADS, start_local, 0)

    neighbours = [jnp.where(has, 1, 0) for has in row_has + col_has]
    pl.semaphore_wait(barrier, 3 + sum(neighbours))
    for h in range(LEAD):
        own_first(h, 0).start()
        own_first(h, 1).start()
    for h in range(LEAD):
        q_copy(h).wait()
        q_send(h).start()

    place = lax.broadcasted_iota(jnp.int32, (16, QN), 0)
    source = place >> 2
    step = jnp.where(source == 0, 0, jnp.where(source == 1, 3, jnp.where(source == 2, 1, 2)))
    base = ((x + step) & 3) * (2 * SLOTS) + (place & 3)
    for ref, half in ((bias_own, yh), (bias_out, 1 - yh)):
        target = base + half * SLOTS
        count = jnp.zeros((16, QN), jnp.int32)
        for j in range(CTX):
            listed = owner_ref[j] * SLOTS + slot_ref[j]
            listed = jnp.where(j // BPC < span_ref[0], listed, -1)
            count = count + jnp.where(target == listed, 1, 0)
        ref[...] = jnp.where(count == 0, NONE, jnp.where(count == 1, 0.0, TWICE)).astype(jnp.float32)

    bias_send.start()
    for h in range(LEAD):
        cache_copy(h).wait()
    k_copy.wait()
    v_copy.wait()
    for c in range(CHUNKS):
        for way in range(2):
            pl.when(row_to[way])(row_send(c, way).start)

    def fill_edges_and_select():
        for way, ref in ((0, kv_up), (1, kv_dn)):

            @pl.when(jnp.logical_not(row_has[way]))
            def _():
                ref[...] = jnp.zeros_like(ref)

        for way in range(2):

            @pl.when(jnp.logical_not(col_has[way]))
            def _():
                strip_in[way] = jnp.zeros(strip_in.shape[1:], strip_in.dtype)

        strip_row = lax.broadcasted_iota(jnp.int32, (STRIP, 512), 0)
        from_row = lax.broadcasted_iota(jnp.int32, (STRIP, 512), 1)
        frame = (strip_row >> 4) & 3
        height = strip_row & 15
        for way in range(2):
            column = (strip_row >> 6) + (5 if way == 0 else 0)
            wanted = jnp.where(
                height < 4,
                256 + frame * 32 + height * 8,
                jnp.where(height < 12, frame * 64 + (height - 4) * 8, 384 + frame * 32 + (height - 12) * 8),
            )
            select[way] = jnp.where(wanted + column == from_row, 1.0, 0.0).astype(jnp.bfloat16)

    def mask_part(first, count, row_col):
        r = lax.broadcasted_iota(jnp.int32, (count, QN), 0)
        query = lax.broadcasted_iota(jnp.int32, (count, QN), 1)
        row, col = row_col(r)
        down = row - ((query >> 3) & 7)
        right = col - (query & 7)
        row_at = row + sy * 8
        col_at = col + sx * 8
        near = (down <= REACH) & (down >= -REACH) & (right <= REACH) & (right >= -REACH)
        inside = (row_at >= 0) & (row_at < rows_n * 8) & (col_at >= 0) & (col_at < cols_n * 8)
        mask[first : first + count, :] = jnp.where(near & inside, 0.0, NONE).astype(jnp.float32)

    def make_mask():
        mask_part(0, 256, lambda r: ((r >> 3) & 7, r & 7))
        mask_part(256, 128, lambda r: (((r >> 3) & 3) - 4, r & 7))
        mask_part(384, 128, lambda r: (((r >> 3) & 3) + 8, r & 7))
        mask_part(512, STRIP, lambda r: ((r & 15) - 4, (r >> 6) - 3))
        mask_part(512 + STRIP, STRIP, lambda r: ((r & 15) - 4, (r >> 6) + 8))

    def ring_scores(h, query, bias, blocks):
        scores, highest = [], jnp.full((1, QN), FLOOR, jnp.float32)
        for r in blocks:
            s = dot(land[h, r, :, 0].reshape(QN, HEAD), query, NT)
            for b in range(4):
                top = jnp.max(s[b * BLK : (b + 1) * BLK], axis=0, keepdims=True)
                highest = jnp.maximum(highest, top + bias[4 * r + b : 4 * r + b + 1])
            scores.append(s)
        return scores, highest

    def ring_sums(h, scores, highest, bias, blocks, total, mixed):
        for r, s in zip(blocks, scores):
            shift = [highest - bias[4 * r + b : 4 * r + b + 1] for b in range(4)]
            p = jnp.concatenate([jnp.exp2((s[b * BLK : (b + 1) * BLK] - shift[b]) * RATE) for b in range(4)], 0)
            total = total + jnp.sum(p, axis=0, keepdims=True)
            mixed = mixed + dot(land[h, r, :, 1].reshape(QN, HEAD), p.astype(jnp.bfloat16), TN)
        return total, mixed

    def no_sum():
        return jnp.zeros((1, QN), jnp.float32), jnp.zeros((HEAD, QN), jnp.float32)

    def far_early(h):
        bias = bias_far[...]
        scores, highest = ring_scores(h, q_far[h], bias, (0, 1, 2))
        total, mixed = ring_sums(h, scores, highest, bias, (0, 1, 2), *no_sum())
        at = lax.rem(h, LAG + 1)
        far_sum[at] = mixed
        far_stat[at, 0:1] = highest
        far_stat[at, 1:2] = total

    def far_late(h):
        bias = bias_far[...]
        at = lax.rem(h, LAG + 1)
        early_highest, early_total = far_stat[at, 0:1], far_stat[at, 1:2]
        scores, highest = ring_scores(h, q_far[h], bias, (3,))
        highest = jnp.maximum(highest, early_highest).astype(jnp.bfloat16).astype(jnp.float32)
        early = jnp.exp2((early_highest - highest) * RATE)
        total, mixed = ring_sums(h, scores, highest, bias, (3,), early_total * early, far_sum[at] * early)
        coarse = total.astype(jnp.bfloat16).astype(jnp.float32)
        row = lax.broadcasted_iota(jnp.int32, (16, QN), 0)
        stats = jnp.where(row == 0, highest, jnp.where(row == 1, coarse, total - coarse))
        part_out[h, :HEAD] = mixed.astype(jnp.bfloat16)
        part_out[h, HEAD:] = stats.astype(jnp.bfloat16)

    def attend_own(h):
        query = q_own[h]
        bias = bias_own[...]
        c = h // (HEADS // CHUNKS)
        here = lanes(h - c * (HEADS // CHUNKS))

        def pieces(kv):
            own = kv_own[kv, :, :, lanes(h)].reshape(QN, HEAD)
            up = kv_up[c, kv, :, :, here].reshape(128, HEAD)
            dn = kv_dn[c, kv, :, :, here].reshape(128, HEAD)
            left = strip_in[0, c, kv, :, here]
            right = strip_in[1, c, kv, :, here]
            return own, jnp.concatenate([up, dn], 0), jnp.concatenate([left, right], 0)

        blocks = (0, 1, 2, 3)
        scores, highest = ring_scores(h, query, bias, blocks)
        near, first = [], 0
        for piece in pieces(0):
            s = dot(piece, query, NT) + mask[first : first + piece.shape[0], :]
            first += piece.shape[0]
            highest = jnp.maximum(highest, jnp.max(s, axis=0, keepdims=True))
            near.append(s)
        total, mixed = ring_sums(h, scores, highest, bias, blocks, *no_sum())
        for piece, s in zip(pieces(1), near):
            p = jnp.exp2((s - highest) * RATE)
            total = total + jnp.sum(p, axis=0, keepdims=True)
            mixed = mixed + dot(piece, p.astype(jnp.bfloat16), TN)
        own_sum[h] = mixed
        own_stat[h, 0:1] = highest
        own_stat[h, 1:2] = total

    def merge(h):
        part_send(h).wait_recv()
        stats = part_in[h, HEAD:].astype(jnp.float32)
        far_highest, far_total = stats[0:1], stats[1:2] + stats[2:3]
        highest, total = own_stat[h, 0:1], own_stat[h, 1:2]
        top = jnp.maximum(highest, far_highest)
        here_scale = jnp.exp2((highest - top) * RATE)
        far_scale = jnp.exp2((far_highest - top) * RATE)
        inverse = 1.0 / (total * here_scale + far_total * far_scale)
        result = own_sum[h] * (here_scale * inverse) + part_in[h, :HEAD].astype(jnp.float32) * (far_scale * inverse)
        out_ref[:, lanes(h)] = result.T.astype(jnp.bfloat16)

    def make_strips(c):
        for way in range(2):
            pl.when(row_has[way])(row_send(c, way).wait_recv)
        for kv in range(2):
            tile = kv_own[kv, :, :, lanes(c, CW)].reshape(QN, CW)
            halo = jnp.concatenate([kv_up[c, kv].reshape(128, CW), kv_dn[c, kv].reshape(128, CW)], 0)
            for way in range(2):
                packed = jnp.dot(select[way, :, :QN], tile, preferred_element_type=jnp.float32)
                packed = packed + jnp.dot(select[way, :, QN:], halo, preferred_element_type=jnp.float32)
                strip_out[way, c, kv] = packed.astype(jnp.bfloat16)
        for way in range(2):
            pl.when(col_to[way])(col_send(c, way).start)

    def ring_step(h, carry):
        @pl.when(h < HEADS)
        def _():
            for way in range(2):
                own_send(h, way).wait_recv()
                forward(h, way).start()

        def send_step(i, carry):
            cache_copy(i).wait()
            own_send(i, 0).start()
            own_send(i, 1).start()
            return carry

        lax.fori_loop(sent(h), sent(h + 1), send_step, 0)

        @pl.when(h + LEAD < HEADS)
        def _():
            q_copy(h + LEAD).wait()
            q_send(h + LEAD).start()

        pl.when(h == 0)(fill_edges_and_select)
        pl.when(h == 1)(make_mask)

        @pl.when((h >= 2) & (h < 2 + CHUNKS))
        def _():
            make_strips(h - 2)

        @pl.when(h >= LAG)
        def _():
            for way in range(2):
                forward(h - LAG, way).wait_recv()
            far_late(h - LAG)
            part_send(h - LAG).start()

        @pl.when(h < HEADS)
        def _():
            q_send(h).wait_recv()
            pl.when(h == 0)(bias_send.wait_recv)
            far_early(h)

        def merge_step(i, carry):
            merge(i)
            return carry

        def own_step(i, carry):
            @pl.when(lax.rem(i, HEADS // CHUNKS) == 0)
            def _():
                for way in range(2):
                    pl.when(col_has[way])(col_send(i // (HEADS // CHUNKS), way).wait_recv)

            attend_own(i)
            return carry

        lax.fori_loop(own_done(h - MERGE_LAG), own_done(h - MERGE_LAG + 1), merge_step, 0)
        lax.fori_loop(own_done(h), own_done(h + 1), own_step, 0)
        return carry

    def sent(step):
        return jnp.minimum(jnp.minimum(step + LEAD, jnp.maximum(EARLY, step + LAST_LEAD)), HEADS)

    def own_done(step):
        caught_up = jnp.clip(2 * (step - FIRST_OWN), 0, jnp.maximum(step - LAG - 1, 0))
        return jnp.where(step >= steps, HEADS, caught_up)

    steps = HEADS + LAG
    lax.fori_loop(0, steps, ring_step, 0)
    for h in range(HEADS - MERGE_LAG - 1, HEADS - 1):
        merge(h)

    def finish(h, carry):
        for way in range(2):
            own_send(h, way).wait_send()
            forward(h, way).wait_send()
        q_send(h).wait_send()
        part_send(h).wait_send()
        return carry

    lax.fori_loop(0, HEADS, finish, 0)
    bias_send.wait_send()
    for c in range(CHUNKS):
        for way in range(2):
            pl.when(row_to[way])(row_send(c, way).wait_send)
            pl.when(col_to[way])(col_send(c, way).wait_send)
    merge(HEADS - 1)


def per_device(queries, keys, values, cache, ctx_owner, ctx_slot, span_count):
    bf16, f32, dma = jnp.bfloat16, jnp.float32, pltpu.SemaphoreType.DMA
    smem = pl.BlockSpec(memory_space=pltpu.SMEM)
    anywhere = pl.BlockSpec(memory_space=pl.ANY)
    attended = pl.pallas_call(
        kernel,
        out_shape=pltpu.VMEM((QN, HD), bf16),
        in_specs=[smem] * 3 + [anywhere] * 4,
        out_specs=pl.BlockSpec(memory_space=pltpu.VMEM),
        scratch_shapes=[
            pltpu.VMEM((HEADS, 4, SLOTS, 2, BLK, HEAD), bf16),
            pltpu.VMEM((HEADS, QN, HEAD), bf16),
            pltpu.VMEM((HEADS, QN, HEAD), bf16),
            pltpu.VMEM((2, FRAMES, 64, HD), bf16),
            pltpu.VMEM((CHUNKS, 2, FRAMES, 32, CW), bf16),
            pltpu.VMEM((CHUNKS, 2, FRAMES, 32, CW), bf16),
            pltpu.VMEM((2, CHUNKS, 2, STRIP, CW), bf16),
            pltpu.VMEM((2, CHUNKS, 2, STRIP, CW), bf16),
            pltpu.VMEM((2, STRIP, 512), bf16),
            pltpu.VMEM((512 + 2 * STRIP, QN), f32),
            pltpu.VMEM((16, QN), f32),
            pltpu.VMEM((16, QN), f32),
            pltpu.VMEM((16, QN), f32),
            pltpu.VMEM((HEADS, HEAD + 16, QN), bf16),
            pltpu.VMEM((HEADS, HEAD + 16, QN), bf16),
            pltpu.VMEM((LAG + 1, HEAD, QN), f32),
            pltpu.VMEM((LAG + 1, 8, QN), f32),
            pltpu.VMEM((HEADS, HEAD, QN), f32),
            pltpu.VMEM((HEADS, 8, QN), f32),
            dma((HEADS,)), dma((HEADS,)), dma((2,)),
            dma((2, HEADS)), dma((2, HEADS)), dma((2, HEADS)), dma((2, HEADS)),
            dma((HEADS,)), dma((HEADS,)), dma((HEADS,)), dma((HEADS,)),
            dma, dma,
            dma((2, CHUNKS)), dma((2, CHUNKS)), dma((2, CHUNKS)), dma((2, CHUNKS)),
        ],
        compiler_params=pltpu.CompilerParams(
            collective_id=0, has_side_effects=True, vmem_limit_bytes=60 * 2**20
        ),
        cost_estimate=pl.CostEstimate(flops=4 * QN * 2944 * HD, bytes_accessed=6 * 2**20, transcendentals=QN * 2944 * HEADS),
        name="span_attention",
    )(
        ctx_owner.reshape(-1),
        ctx_slot.reshape(-1),
        span_count.reshape(-1),
        queries.reshape(QN, HD),
        keys.reshape(FRAMES, 64, HD),
        values.reshape(FRAMES, 64, HD),
        cache.reshape(SLOTS, 2, BLK, HD),
    )
    return attended.reshape(queries.shape)


def solution(mesh):
    placed = (
        P("clip", None, "sy", "sx", None),
        P("clip", None, "sy", "sx", None),
        P("clip", None, "sy", "sx", None),
        P("clip", "sy", "sx", None, None, None),
        P("clip", "sy", "sx", None),
        P("clip", "sy", "sx", None),
        P("clip"),
    )
    return jax.shard_map(
        per_device,
        mesh=mesh,
        in_specs=placed,
        out_specs=P("clip", None, "sy", "sx", None),
        check_vma=False,
    )
```
